256 devices in a mesh: dp: 64 (over x, z, core), sp: 4 (over y).
Axes of the slice: x: 4, y: 4, z: 8, core: 2. Of those that a mesh axis runs over, the one named last changes fastest.
Arguments:
- base_query: bfloat16 [64, 1024, 4096], P('dp', 'sp'), may hold values from -8 to 8
- base_key: bfloat16 [64, 1024, 512], P('dp', 'sp'), may hold values from -8 to 8
- reference_value_rows: bfloat16 [64, 1024, 512], P('dp', 'sp'), may hold values from -6 to 6
- actor_query: bfloat16 [64, 1024, 4096], P('dp', 'sp'), may hold values from -8 to 8
- actor_key: bfloat16 [64, 1024, 512], P('dp', 'sp'), may hold values from -8 to 8
- actor_value_rows: bfloat16 [64, 1024, 512], P('dp', 'sp'), may hold values from -6 to 6
- segment_labels: int32 [64, 1024], P('dp', 'sp'), may hold values from 0 to 2, never falling along the last dimension, each value on 1 to 512 neighbouring positions
- shard_plan: int32 [64], replicated, may hold values from 0 to 63, each once
Outputs:
- base_output: bfloat16 [64, 1024, 4096], P('dp', 'sp')
- actor_output: bfloat16 [64, 1024, 4096], P('dp', 'sp')
The draws below stay inside these ranges and needn't reach their ends.
Inputs may be any that keep to these rules, and one draw needn't show every extreme that they name: `segment_labels`: along an owner's rows the labels never decrease; a response has 1 to 512 rows, and some response has exactly 512. `shard_plan`: each group is named by exactly one owner.
All inputs are finite; a program needn't handle non-finite values.
Results may differ from the reference program's by a relative error of at most 0.0079.
Values may be sent and summed in bfloat16 or wider, within the bound.
No kernel may reach another device: no remote copies, remote signals or barrier semaphores. Data moves between devices by JAX's collectives and lax.ppermute only.
A program may use at most 128 MiB of HBM per device.

```python
import math
import jax
import jax.numpy as jnp
import numpy as np
from jax import lax

QUERY_HEADS = 32
KEY_VALUE_HEADS = 4
HEAD_SIZE = 128
SEGS = 3
OWNER_COUNT = 64
OWNER_ROWS = 1024


def drawn_normal(key, head_count):
    return jnp.clip(jax.random.normal(key, (OWNER_COUNT, OWNER_ROWS, head_count * HEAD_SIZE), dtype=jnp.float32), -6.0, 6.0)


def draw_base_query(key, part):
    key = jax.random.fold_in(key, 11)
    return drawn_normal(key, QUERY_HEADS).astype(jnp.bfloat16)


def draw_base_key(key, part):
    key = jax.random.fold_in(key, 12)
    return drawn_normal(key, KEY_VALUE_HEADS).astype(jnp.bfloat16)


def draw_actor_query(key, part):
    key = jax.random.fold_in(key, 13)
    return drawn_normal(key, QUERY_HEADS).astype(jnp.bfloat16)


def draw_actor_key(key, part):
    key = jax.random.fold_in(key, 14)
    return drawn_normal(key, KEY_VALUE_HEADS).astype(jnp.bfloat16)


def steps_of(key, shape, shards, smallest, top_value):
    def one(dim, shards_of):
        steps = jax.random.uniform(jax.random.fold_in(jax.random.fold_in(key, 6), dim), (shards_of,), jnp.float32, smallest / len(shards), top_value / len(shards))
        return jnp.repeat(jnp.exp(steps), shape[dim] // shards_of).reshape((-1,) + (1,) * (len(shape) - dim - 1))

    factor_of = one(*shards[0])
    for cut in shards[1:]:
        factor_of = factor_of * one(*cut)
    return factor_of


def length_profile(number_of, total, reach, slope):
    weights = [(1 << 20) // math.isqrt(rank ** slope) + 1 for rank in range(2, number_of + 1)]
    surplus, given = total - reach - (number_of - 1), [1] * (number_of - 1)
    while surplus > 0:
        movable = [i for i in range(number_of - 1) if given[i] < reach]
        pool, left = sum([weights[i] for i in movable]), surplus
        for i in movable:
            extra = min(reach - given[i], max(1, left * weights[i] // pool), surplus)
            given[i] = given[i] + extra
            surplus = surplus - extra
    return np.array([reach] + given)


def uneven(rng, amount, total, reach, lean):
    if amount == 2:
        one = jax.random.randint(rng, (), max(1, total - reach), min(reach, total - 1) + 1)
        return jnp.stack([one, total - one])
    sizes = jnp.asarray(length_profile(amount, total, reach, lean), jnp.int32)
    couples = (amount - 1) // 2
    donor, taker = sizes[1:1 + 2 * couples:2], sizes[2:2 + 2 * couples:2]
    margin = jnp.minimum(donor - 1, reach - taker)
    passed = jax.random.randint(jax.random.fold_in(rng, 1), (couples,), 0, 1 << 20) % (margin + 1)
    sizes = sizes.at[1:1 + 2 * couples:2].set(donor - passed).at[2:2 + 2 * couples:2].set(taker + passed)
    return sizes[jax.random.permutation(jax.random.fold_in(rng, 2), amount)]


def noise(key, shape, width, limit, cuts=(), kind=jnp.bfloat16):
    drawn = jax.random.normal(key, shape, jnp.float32) * width
    if len(cuts) > 0:
        drawn = steps_of(key, shape, cuts, -0.22, 0.18) * drawn
    return jnp.clip(drawn, min=-limit, max=limit).astype(kind)


def setup_inputs(seed: int = 0) -> dict:
    streams_of = jax.random.split(jax.random.key(seed), 9)
    base_query = draw_base_query(jax.random.fold_in(streams_of[8], 71), 0)
    base_key = draw_base_key(jax.random.fold_in(streams_of[8], 71), 0)
    reference_value_rows = noise(streams_of[2], (OWNER_COUNT, OWNER_ROWS, KEY_VALUE_HEADS * HEAD_SIZE), 1.0, 6.0, ((0, 64), (1, 4)))
    actor_query = draw_actor_query(jax.random.fold_in(streams_of[8], 71), 0)
    actor_key = draw_actor_key(jax.random.fold_in(streams_of[8], 71), 0)
    actor_value_rows = noise(streams_of[5], (OWNER_COUNT, OWNER_ROWS, KEY_VALUE_HEADS * HEAD_SIZE), 1.0, 6.0, ((0, 64), (1, 4)))
    segment_labels = jax.vmap(lambda own: jnp.searchsorted(jnp.cumsum(uneven(own, SEGS, OWNER_ROWS, OWNER_ROWS // 2, 2)), jnp.arange(OWNER_ROWS), side="right"))(jax.random.split(streams_of[6], OWNER_COUNT)).reshape((OWNER_COUNT, OWNER_ROWS)).astype(jnp.int32)
    shard_plan = jax.random.permutation(streams_of[7], OWNER_COUNT).astype(jnp.int32)
    return dict(base_query=base_query, base_key=base_key, reference_value_rows=reference_value_rows, actor_query=actor_query, actor_key=actor_key, actor_value_rows=actor_value_rows, segment_labels=segment_labels, shard_plan=shard_plan)


theta_base = 1000000.0

def response_places(labels):
    column_height = labels.shape[0]
    segment_ids = jnp.arange(SEGS).astype(jnp.int32)
    member_table = (labels[:, None] == segment_ids[None, :]).astype(jnp.int32)
    sizes = lax.optimization_barrier(jnp.sum(member_table, axis=0))
    starts = jnp.cumsum(sizes) - sizes
    row_start = lax.optimization_barrier(jnp.sum(member_table * starts[None, :], axis=1))
    return (jnp.arange(column_height).astype(jnp.int32) - row_start).astype(jnp.float32)

def apply_rotary(value_tensor, head_count, head_width, row_positions):
    column_height = value_tensor.shape[0]
    half_width = head_width // 2
    rate_table = jnp.exp(jnp.arange(half_width).astype(jnp.float32) * (-2.0 * math.log(theta_base) / head_width))
    angles = row_positions[:, None] * rate_table[None, :]
    cosine = jnp.cos(angles)[:, None, :]
    sine_part = jnp.sin(angles)[:, None, :]
    shaped = value_tensor.astype(jnp.float32).reshape(column_height, head_count, head_width)
    leading = shaped[:, :, :half_width]
    trailing = shaped[:, :, half_width:]
    turned = jnp.concatenate([leading * cosine - trailing * sine_part, trailing * cosine + leading * sine_part], axis=-1)
    return turned.reshape(column_height, head_count * head_width).astype(jnp.bfloat16)

def attend(queries, key_tensor, value_tensor, labels):
    column_height = queries.shape[0]
    group_span_width = QUERY_HEADS // KEY_VALUE_HEADS
    rows_per_block = min(512, column_height)
    heads_of_keys = key_tensor.astype(jnp.float32).reshape(column_height, KEY_VALUE_HEADS, HEAD_SIZE)
    heads_of_values = value_tensor.astype(jnp.float32).reshape(column_height, KEY_VALUE_HEADS, HEAD_SIZE)
    key_places = jnp.arange(column_height).astype(jnp.int32)
    scaling = 1.0 / math.sqrt(HEAD_SIZE)

    def one_block(block_index):
        start_row = (block_index * rows_per_block).astype(jnp.int32)
        block_of_queries = lax.dynamic_slice_in_dim(queries, start_row, rows_per_block, 0).astype(jnp.float32)
        block_of_queries = block_of_queries.reshape(rows_per_block, KEY_VALUE_HEADS, group_span_width, HEAD_SIZE)
        label_block = lax.dynamic_slice_in_dim(labels, start_row, rows_per_block, 0)
        scores = jnp.einsum('qhgd,khd->hgqk', block_of_queries, heads_of_keys) * scaling
        query_places = start_row + jnp.arange(rows_per_block).astype(jnp.int32)
        allowed = (label_block[:, None] == labels[None, :]) & (key_places[None, :] <= query_places[:, None])
        scores = jnp.where(allowed, scores, -jnp.inf)
        row_peak = lax.optimization_barrier(jnp.max(scores, axis=-1, keepdims=True))
        raised = jnp.exp(scores - row_peak)
        totals = lax.optimization_barrier(jnp.sum(raised, axis=-1, keepdims=True))
        weights = (raised / totals).astype(jnp.bfloat16)
        blended = jnp.einsum('hgqk,khd->qhgd', weights.astype(jnp.float32), heads_of_values)
        return blended.reshape(rows_per_block, QUERY_HEADS * HEAD_SIZE).astype(jnp.bfloat16)
    blocks = lax.map(one_block, jnp.arange(column_height // rows_per_block).astype(jnp.int32))
    return blocks.reshape(column_height, QUERY_HEADS * HEAD_SIZE)

def reference(base_query, base_key, reference_value_rows, actor_query, actor_key, actor_value_rows, segment_labels, shard_plan):

    def policy_pass(queries, key_tensor, value_tensor):

        def one_owner(inputs):
            owner_queries, keys_per_owner, owner_values, owner_labels = inputs
            row_positions = response_places(owner_labels)
            turned_queries = apply_rotary(owner_queries, QUERY_HEADS, HEAD_SIZE, row_positions)
            keys_after_rotary = apply_rotary(keys_per_owner, KEY_VALUE_HEADS, HEAD_SIZE, row_positions)
            return attend(turned_queries, keys_after_rotary, owner_values, owner_labels)
        return lax.map(one_owner, (queries, key_tensor, value_tensor, segment_labels))
    base_output = policy_pass(base_query, base_key, reference_value_rows)
    actor_home = policy_pass(actor_query, actor_key, actor_value_rows)
    owner_index = jnp.arange(OWNER_COUNT).astype(jnp.int32)
    source_owner = lax.optimization_barrier(jnp.sum(owner_index[:, None] * (shard_plan[:, None] == owner_index[None, :]).astype(jnp.int32), axis=0))
    actor_output = jnp.take(actor_home, source_owner, axis=0)
    return (base_output, actor_output)
```

```python
import functools
import math

import jax
import jax.numpy as jnp
import numpy as np
from jax import lax
from jax.experimental import pallas as pl
from jax.experimental.pallas import tpu as pltpu
from jax.sharding import PartitionSpec as P

QUERY_HEADS = 32
KEY_VALUE_HEADS = 4
HEAD_SIZE = 128
GROUP = QUERY_HEADS // KEY_VALUE_HEADS
SEGS = 3
THETA = 1000000.0
ROWS = 256
OWNERS = 64
LEAD = 1
SCALE = math.log2(math.e) / math.sqrt(HEAD_SIZE)
MASKED = -1e30
BF = jnp.bfloat16
F32 = jnp.float32


def angle_tables():
    half = HEAD_SIZE // 2
    rate = THETA ** (-2.0 * np.arange(half) / HEAD_SIZE)
    angle = np.arange(3 * ROWS)[:, None] * np.concatenate([rate, rate])[None, :]
    return np.cos(angle).astype(np.float32), np.sin(angle).astype(np.float32)


def pack_first_kernel(k_ref, v_ref, lab_ref, first_ref, rest_ref):
    width = LEAD * 256
    for c in range(KEY_VALUE_HEADS):
        k = k_ref[:, c * 128 : (c + 1) * 128]
        v = v_ref[:, c * 128 : (c + 1) * 128]
        if c < LEAD:
            first_ref[0:ROWS, c * 256 : c * 256 + 128] = k
            first_ref[0:ROWS, c * 256 + 128 : c * 256 + 256] = v
        else:
            rest_ref[:, (c - LEAD) * 256 : (c - LEAD) * 256 + 128] = k
            rest_ref[:, (c - LEAD) * 256 + 128 : (c - LEAD) * 256 + 256] = v
    along = (lab_ref[...] + 1).astype(F32)
    down = jnp.transpose(jnp.broadcast_to(along, (128, ROWS)))
    first_ref[0:ROWS, width : width + 128] = down.astype(BF)
    first_ref[ROWS : ROWS + 16, :] = jnp.zeros((16, width + 128), BF)
    first_ref[ROWS : ROWS + 16, 0:ROWS] = jnp.broadcast_to(along, (16, ROWS)).astype(BF)


def pack_first(k, v, labels):
    return pl.pallas_call(
        pack_first_kernel,
        out_shape=(
            jax.ShapeDtypeStruct((ROWS + 16, LEAD * 256 + 128), BF),
            jax.ShapeDtypeStruct((ROWS, (KEY_VALUE_HEADS - LEAD) * 256), BF),
        ),
        compiler_params=pltpu.CompilerParams(vmem_limit_bytes=16 << 20),
    )(k, v, labels)


def pack_plain_kernel(k_ref, v_ref, out_ref):
    for c in range(KEY_VALUE_HEADS):
        out_ref[:, c * 256 : c * 256 + 128] = k_ref[:, c * 128 : (c + 1) * 128]
        out_ref[:, c * 256 + 128 : c * 256 + 256] = v_ref[:, c * 128 : (c + 1) * 128]


def pack_plain(k, v):
    return pl.pallas_call(
        pack_plain_kernel,
        out_shape=jax.ShapeDtypeStruct((ROWS, KEY_VALUE_HEADS * 256), BF),
        compiler_params=pltpu.CompilerParams(vmem_limit_bytes=16 << 20),
    )(k, v)


def from_previous(x, size, step):
    return lax.ppermute(x, "sp", [(i, i + step) for i in range(size - step)])


def rotate(x, cosine, sine):
    x = x.astype(F32)
    return (x * cosine + pltpu.roll(x, HEAD_SIZE // 2, 1) * sine).astype(BF)


def attend_kernel(
    pieces,
    q_ref,
    kv0_ref,
    kv1_ref,
    kv2_ref,
    down0_ref,
    down1_ref,
    down2_ref,
    along0_ref,
    along1_ref,
    along2_ref,
    cos_ref,
    sin_ref,
    out_ref,
    turn_cos,
    turn_sin,
    bias_near,
    bias_ends,
):
    within = lax.broadcasted_iota(jnp.int32, (ROWS, ROWS), 1) <= lax.broadcasted_iota(
        jnp.int32, (ROWS, ROWS), 0
    )

    @pl.when(pl.program_id(0) == 0)
    def _():
        along = [ref[0:1, :].astype(F32) for ref in (along2_ref, along1_ref, along0_ref)]
        down = [ref[...].astype(F32) for ref in (down2_ref, down1_ref, down0_ref)]
        place = lax.broadcasted_iota(jnp.int32, (1, ROWS), 1)
        starts = []
        for label in range(1, SEGS + 1):
            least = jnp.full((1, ROWS), 3 * ROWS - 1, jnp.int32)
            for b in range(3):
                least = jnp.minimum(
                    least, jnp.where(along[b] == label, place + b * ROWS, 3 * ROWS - 1)
                )
            starts.append(jnp.min(least))
        start_cos = [cos_ref[pl.ds(s, 1), :] for s in starts]
        start_sin = [sin_ref[pl.ds(s, 1), :] for s in starts]
        sign = jnp.where(
            lax.broadcasted_iota(jnp.int32, (1, HEAD_SIZE), 1) < HEAD_SIZE // 2, -1.0, 1.0
        )
        for b in range(3):
            rows = pl.ds(b * ROWS, ROWS)
            first, second = down[b] == 1, down[b] == 2
            sc = jnp.where(first, start_cos[0], jnp.where(second, start_cos[1], start_cos[2]))
            ss = jnp.where(first, start_sin[0], jnp.where(second, start_sin[1], start_sin[2]))
            ic, isn = cos_ref[rows, :], sin_ref[rows, :]
            turn_cos[rows, :] = ic * sc + isn * ss
            turn_sin[rows, :] = (isn * sc - ic * ss) * sign
        own = jnp.concatenate([down[2], down[2]], axis=1)
        bias_near[...] = jnp.where(along[1] == own, 0.0, MASKED)
        bias_ends[...] = jnp.where(jnp.where(within, along[2], along[0]) == own, 0.0, MASKED)

    keys, values = [], []
    ones = jnp.ones((ROWS, HEAD_SIZE), BF)
    for b, ref in enumerate((kv2_ref, kv1_ref, kv0_ref)):
        rows = pl.ds(b * ROWS, ROWS)
        keys.append(rotate(ref[0:ROWS, 0:128], turn_cos[rows, :], turn_sin[rows, :]))
        values.append(jnp.concatenate([ref[0:ROWS, 128:256], ones], axis=1))
    keys = jnp.concatenate(keys, axis=0)
    values = jnp.concatenate(values, axis=0)
    own_cos = turn_cos[pl.ds(2 * ROWS, ROWS), :]
    own_sin = turn_sin[pl.ds(2 * ROWS, ROWS), :]
    for h in range(GROUP):
        q = rotate(q_ref[:, h * 128 : (h + 1) * 128], own_cos, own_sin)
        s = lax.dot_general(q, keys, (((1,), (1,)), ((), ())), preferred_element_type=F32)
        ends = jnp.where(within, s[:, 2 * ROWS :], s[:, :ROWS]) * SCALE + bias_ends[...]
        near = s[:, ROWS : 2 * ROWS] * SCALE + bias_near[...]
        peak = jnp.max(jnp.maximum(ends, near), axis=1, keepdims=True)
        ends = jnp.exp2(ends - peak)
        near = jnp.exp2(near - peak).astype(BF)
        inner = jnp.where(within, ends, 0.0).astype(BF)
        outer = jnp.where(within, 0.0, ends).astype(BF)
        weights = jnp.concatenate([outer, near, inner], axis=1)
        o = jnp.dot(weights, values, preferred_element_type=F32)
        o = (o[:, :128] / o[:, 128:]).astype(BF)
        if pieces:
            lanes = slice((h % 2) * 128, (h % 2) * 128 + 128)
            out_ref[:, h // 2, :, lanes] = o.reshape(16, 16, 128)
        else:
            out_ref[:, h * 128 : (h + 1) * 128] = o


def attend(pieces, q, first, count, kvs, lab, tables):
    width = LEAD * 256
    specs = [pl.BlockSpec((ROWS, GROUP * 128), lambda c: (0, c + first))]
    specs += [pl.BlockSpec((ROWS, 256), lambda c: (0, c))] * 3
    specs += [pl.BlockSpec((ROWS, 128), lambda c: (0, width // 128))] * 3
    specs += [pl.BlockSpec((16, ROWS), lambda c: (ROWS // 16, 0))] * 3
    specs += [pl.BlockSpec((3 * ROWS, HEAD_SIZE), lambda c: (0, 0))] * 2
    if pieces:
        out_shape = jax.ShapeDtypeStruct((16, 4, 16, count * 256), BF)
        out_spec = pl.BlockSpec((16, 4, 16, 256), lambda c: (0, 0, 0, c))
    else:
        out_shape = jax.ShapeDtypeStruct((ROWS, QUERY_HEADS * HEAD_SIZE), BF)
        out_spec = pl.BlockSpec((ROWS, GROUP * 128), lambda c: (0, c + first))
    return pl.pallas_call(
        functools.partial(attend_kernel, pieces),
        grid=(count,),
        in_specs=specs,
        out_specs=out_spec,
        out_shape=out_shape,
        scratch_shapes=[
            pltpu.VMEM((3 * ROWS, HEAD_SIZE), F32),
            pltpu.VMEM((3 * ROWS, HEAD_SIZE), F32),
            pltpu.VMEM((ROWS, ROWS), F32),
            pltpu.VMEM((ROWS, ROWS), F32),
        ],
        compiler_params=pltpu.CompilerParams(vmem_limit_bytes=32 << 20),
        cost_estimate=pl.CostEstimate(
            flops=count * GROUP * 4 * ROWS * 3 * ROWS * HEAD_SIZE,
            bytes_accessed=count * ROWS * (GROUP * 256 * 2 + 3 * 512),
            transcendentals=count * GROUP * ROWS * 2 * ROWS,
        ),
    )(q, *kvs, *lab, *lab, *tables)


def pick_kernel(plan_ref, lead_ref, rest_ref, out_ref):
    width = LEAD * 256

    def one(u, carry):
        g = plan_ref[u]
        out_ref[g, :, 0:width] = lead_ref[u]
        out_ref[g, :, width:1024] = rest_ref[u]
        return carry

    lax.fori_loop(0, OWNERS, one, 0, unroll=8)


def pick(plan, lead, rest):
    whole = pl.BlockSpec(memory_space=pltpu.VMEM)
    return pl.pallas_call(
        pick_kernel,
        in_specs=[pl.BlockSpec(memory_space=pltpu.SMEM), whole, whole],
        out_specs=whole,
        out_shape=jax.ShapeDtypeStruct((OWNERS, 16, 1024), BF),
        compiler_params=pltpu.CompilerParams(vmem_limit_bytes=16 << 20),
    )(plan, lead, rest)


def lay_kernel(in_ref, out_ref):
    for cb in range(4):
        out_ref[:, :, cb * 256 : (cb + 1) * 256] = in_ref[:, cb]


def lay(arrived):
    out = pl.pallas_call(
        lay_kernel,
        grid=(KEY_VALUE_HEADS,),
        in_specs=[pl.BlockSpec((16, 4, 16, 256), lambda c: (0, 0, 0, c))],
        out_specs=pl.BlockSpec((16, 16, 1024), lambda c: (0, 0, c)),
        out_shape=jax.ShapeDtypeStruct((16, 16, 4096), BF),
        compiler_params=pltpu.CompilerParams(vmem_limit_bytes=16 << 20),
    )(arrived.reshape(16, 4, 16, 1024))
    return out.reshape(ROWS, 4096)


def swap(x):
    return lax.all_to_all(x, "dp", split_axis=0, concat_axis=0, tiled=True)


def per_device(bq, bk, bv, aq, ak, av, labels, plan):
    size = lax.axis_size("sp")
    bq, bk, bv, aq, ak, av = (t[0] for t in (bq, bk, bv, aq, ak, av))
    tables = tuple(jnp.asarray(t) for t in angle_tables())

    head, rest = pack_first(ak, av, labels)
    head1, head2 = (from_previous(head, size, s) for s in (1, 2))
    lab = (head, head1, head2)
    lead = attend(True, aq, 0, LEAD, lab, lab, tables)
    lead = swap(lead.reshape(OWNERS, 16, LEAD * 256))

    rest1, rest2 = (from_previous(rest, size, s) for s in (1, 2))
    others = KEY_VALUE_HEADS - LEAD
    other = attend(True, aq, LEAD, others, (rest, rest1, rest2), lab, tables)
    other = swap(other.reshape(OWNERS, 16, others * 256))

    base = pack_plain(bk, bv)
    base1, base2 = (from_previous(base, size, s) for s in (1, 2))
    base_output = attend(False, bq, 0, KEY_VALUE_HEADS, (base, base1, base2), lab, tables)

    arrived = swap(pick(plan, lead, other))
    return base_output[None], lay(arrived)[None]


def solution(mesh):
    rows = P("dp", "sp", None)
    return jax.shard_map(
        per_device,
        mesh=mesh,
        in_specs=(rows, rows, rows, rows, rows, rows, P("dp", "sp"), P()),
        out_specs=(rows, rows),
        check_vma=False,
    )
```

```python
import functools
import math

import jax
import jax.numpy as jnp
import numpy as np
from jax import lax
from jax.experimental import pallas as pl
from jax.experimental.pallas import tpu as pltpu
from jax.sharding import PartitionSpec as P

QUERY_HEADS = 32
KEY_VALUE_HEADS = 4
HEAD_SIZE = 128
GROUP = QUERY_HEADS // KEY_VALUE_HEADS
SEGS = 3
THETA = 1000000.0
ROWS = 256
OWNERS = 64
LEAD = 1
SCALE = math.log2(math.e) / math.sqrt(HEAD_SIZE)
MASKED = -1e30
BF = jnp.bfloat16
F32 = jnp.float32
SMALL = pltpu.CompilerParams(vmem_limit_bytes=16 << 20)


def in_hbm(x):
    return pltpu.with_memory_space_constraint(x, pltpu.HBM)


def angle_tables():
    half = HEAD_SIZE // 2
    rate = THETA ** (-2.0 * np.arange(half) / HEAD_SIZE)
    angle = np.arange(3 * ROWS)[:, None] * np.concatenate([rate, rate])[None, :]
    return np.cos(angle).astype(np.float32), np.sin(angle).astype(np.float32)


def pack_lead_kernel(k_ref, v_ref, lab_ref, out_ref):
    width = LEAD * 256
    for c in range(LEAD):
        out_ref[0:ROWS, c * 256 : c * 256 + 128] = k_ref[:, c * 128 : (c + 1) * 128]
        out_ref[0:ROWS, c * 256 + 128 : c * 256 + 256] = v_ref[:, c * 128 : (c + 1) * 128]
    along = (lab_ref[...] + 1).astype(F32)
    down = jnp.transpose(jnp.broadcast_to(along, (128, ROWS)))
    out_ref[0:ROWS, width : width + 128] = down.astype(BF)
    out_ref[ROWS : ROWS + 16, ROWS:] = jnp.zeros((16, width + 128 - ROWS), BF)
    out_ref[ROWS : ROWS + 16, 0:ROWS] = jnp.broadcast_to(along, (16, ROWS)).astype(BF)


def pack_lead(k, v, labels):
    half = pl.BlockSpec((ROWS, LEAD * 128), lambda i: (0, 0))
    return pl.pallas_call(
        pack_lead_kernel,
        grid=(1,),
        in_specs=[half, half, pl.BlockSpec((1, ROWS), lambda i: (0, 0))],
        out_specs=pl.BlockSpec((ROWS + 16, LEAD * 256 + 128), lambda i: (0, 0)),
        out_shape=jax.ShapeDtypeStruct((ROWS + 16, LEAD * 256 + 128), BF),
        compiler_params=SMALL,
    )(in_hbm(k), in_hbm(v), in_hbm(labels))


def pack_kernel(first, k_ref, v_ref, out_ref):
    for i, c in enumerate(range(first, KEY_VALUE_HEADS)):
        out_ref[:, i * 256 : i * 256 + 128] = k_ref[:, c * 128 : (c + 1) * 128]
        out_ref[:, i * 256 + 128 : i * 256 + 256] = v_ref[:, c * 128 : (c + 1) * 128]


def pack(k, v, first):
    return pl.pallas_call(
        functools.partial(pack_kernel, first),
        out_shape=jax.ShapeDtypeStruct((ROWS, (KEY_VALUE_HEADS - first) * 256), BF),
        compiler_params=SMALL,
    )(in_hbm(k), in_hbm(v))


def from_previous(x, size, step):
    return lax.ppermute(x, "sp", [(i, (i + step) % size) for i in range(size)])


def rotate(x, cosine, sine):
    x = x.astype(F32)
    return (x * cosine + pltpu.roll(x, HEAD_SIZE // 2, 1) * sine).astype(BF)


def attend_kernel(
    pieces,
    place_ref,
    q_ref,
    kv0_ref,
    kv1_ref,
    kv2_ref,
    down0_ref,
    down1_ref,
    down2_ref,
    along0_ref,
    along1_ref,
    along2_ref,
    cos_ref,
    sin_ref,
    out_ref,
    turn_cos,
    turn_sin,
    bias_near,
    bias_ends,
):
    within = lax.broadcasted_iota(jnp.int32, (ROWS, ROWS), 1) <= lax.broadcasted_iota(
        jnp.int32, (ROWS, ROWS), 0
    )

    @pl.when(pl.program_id(0) == 0)
    def _():
        along = [ref[0:1, :].astype(F32) for ref in (along2_ref, along1_ref, along0_ref)]
        down = [ref[...].astype(F32) for ref in (down2_ref, down1_ref, down0_ref)]
        back = [jnp.where(place_ref[0] >= n, 1.0, 0.0) for n in (2, 1)]
        along = [along[0] * back[0], along[1] * back[1], along[2]]
        down = [down[0] * back[0], down[1] * back[1], down[2]]
        place = lax.broadcasted_iota(jnp.int32, (1, ROWS), 1)
        starts = []
        for label in range(1, SEGS + 1):
            least = jnp.full((1, ROWS), 3 * ROWS - 1, jnp.int32)
            for b in range(3):
                least = jnp.minimum(
                    least, jnp.where(along[b] == label, place + b * ROWS, 3 * ROWS - 1)
                )
            starts.append(jnp.min(least))
        start_cos = [cos_ref[pl.ds(s, 1), :] for s in starts]
        start_sin = [sin_ref[pl.ds(s, 1), :] for s in starts]
        sign = jnp.where(
            lax.broadcasted_iota(jnp.int32, (1, HEAD_SIZE), 1) < HEAD_SIZE // 2, -1.0, 1.0
        )
        for b in range(3):
            rows = pl.ds(b * ROWS, ROWS)
            first, second = down[b] == 1, down[b] == 2
            sc = jnp.where(first, start_cos[0], jnp.where(second, start_cos[1], start_cos[2]))
            ss = jnp.where(first, start_sin[0], jnp.where(second, start_sin[1], start_sin[2]))
            ic, isn = cos_ref[rows, :], sin_ref[rows, :]
            turn_cos[rows, :] = ic * sc + isn * ss
            turn_sin[rows, :] = (isn * sc - ic * ss) * sign
        own = jnp.concatenate([down[2], down[2]], axis=1)
        bias_near[...] = jnp.where(along[1] == own, 0.0, MASKED)
        bias_ends[...] = jnp.where(jnp.where(within, along[2], along[0]) == own, 0.0, MASKED)

    keys, values = [], []
    ones = jnp.ones((ROWS, HEAD_SIZE), BF)
    for b, ref in enumerate((kv2_ref, kv1_ref, kv0_ref)):
        rows = pl.ds(b * ROWS, ROWS)
        keys.append(rotate(ref[0:ROWS, 0:128], turn_cos[rows, :], turn_sin[rows, :]))
        values.append(jnp.concatenate([ref[0:ROWS, 128:256], ones], axis=1))
    keys = jnp.concatenate(keys, axis=0)
    values = jnp.concatenate(values, axis=0)
    own_cos = turn_cos[pl.ds(2 * ROWS, ROWS), :]
    own_sin = turn_sin[pl.ds(2 * ROWS, ROWS), :]
    for h in range(GROUP):
        q = rotate(q_ref[:, h * 128 : (h + 1) * 128], own_cos, own_sin)
        s = lax.dot_general(q, keys, (((1,), (1,)), ((), ())), preferred_element_type=F32)
        ends = jnp.where(within, s[:, 2 * ROWS :], s[:, :ROWS]) * SCALE + bias_ends[...]
        near = s[:, ROWS : 2 * ROWS] * SCALE + bias_near[...]
        peak = jnp.max(jnp.maximum(ends, near), axis=1, keepdims=True)
        ends = jnp.exp2(ends - peak)
        near = jnp.exp2(near - peak).astype(BF)
        inner = jnp.where(within, ends, 0.0).astype(BF)
        outer = jnp.where(within, 0.0, ends).astype(BF)
        weights = jnp.concatenate([outer, near, inner], axis=1)
        o = jnp.dot(weights, values, preferred_element_type=F32)
        o = (o[:, :128] / o[:, 128:]).astype(BF)
        if pieces:
            lanes = slice((h % 2) * 128, (h % 2) * 128 + 128)
            out_ref[:, h // 2, :, lanes] = o.reshape(16, 16, 128)
        else:
            out_ref[:, h * 128 : (h + 1) * 128] = o


def attend(pieces, q, first, count, kvs, lab, tables, weight=1):
    width = LEAD * 256
    specs = [pl.BlockSpec(memory_space=pltpu.SMEM)]
    specs += [pl.BlockSpec((ROWS, GROUP * 128), lambda c: (0, c + first))]
    specs += [pl.BlockSpec((ROWS, 256), lambda c: (0, c))] * 3
    specs += [pl.BlockSpec((ROWS, 128), lambda c: (0, width // 128))] * 3
    specs += [pl.BlockSpec((16, ROWS), lambda c: (ROWS // 16, 0))] * 3
    specs += [pl.BlockSpec((3 * ROWS, HEAD_SIZE), lambda c: (0, 0))] * 2
    if pieces:
        out_shape = pltpu.HBM((16, 4, 16, count * 256), BF)
        out_spec = pl.BlockSpec((16, 4, 16, 256), lambda c: (0, 0, 0, c))
    else:
        out_shape = jax.ShapeDtypeStruct((ROWS, QUERY_HEADS * HEAD_SIZE), BF)
        out_spec = pl.BlockSpec((ROWS, GROUP * 128), lambda c: (0, c + first))
    return pl.pallas_call(
        functools.partial(attend_kernel, pieces),
        grid=(count,),
        in_specs=specs,
        out_specs=out_spec,
        out_shape=out_shape,
        scratch_shapes=[
            pltpu.VMEM((3 * ROWS, HEAD_SIZE), F32),
            pltpu.VMEM((3 * ROWS, HEAD_SIZE), F32),
            pltpu.VMEM((ROWS, ROWS), F32),
            pltpu.VMEM((ROWS, ROWS), F32),
        ],
        compiler_params=pltpu.CompilerParams(vmem_limit_bytes=32 << 20),
        cost_estimate=pl.CostEstimate(
            flops=weight * count * GROUP * 4 * ROWS * 3 * ROWS * HEAD_SIZE,
            bytes_accessed=count * ROWS * (GROUP * 256 * 2 + 3 * 512),
            transcendentals=count * GROUP * ROWS * 2 * ROWS,
        ),
    )(lax.axis_index("sp").astype(jnp.int32)[None], in_hbm(q), *kvs, *lab, *lab, *(in_hbm(t) for t in tables))


def pick_kernel(plan_ref, lead_ref, rest_ref, out_ref):
    def place(ref):
        def one(u, carry):
            out_ref[plan_ref[u]] = ref[u]
            return carry

        lax.fori_loop(0, OWNERS, one, 0, unroll=16)

    @pl.when(pl.program_id(0) < LEAD)
    def _():
        place(lead_ref)

    @pl.when(pl.program_id(0) >= LEAD)
    def _():
        place(rest_ref)


def pick(plan, lead, rest):
    block = (OWNERS, 16, 256)
    return pl.pallas_call(
        pick_kernel,
        grid=(KEY_VALUE_HEADS,),
        in_specs=[
            pl.BlockSpec(memory_space=pltpu.SMEM),
            pl.BlockSpec(block, lambda c: (0, 0, jnp.minimum(c, LEAD - 1))),
            pl.BlockSpec(block, lambda c: (0, 0, jnp.maximum(c - LEAD, 0))),
        ],
        out_specs=pl.BlockSpec(block, lambda c: (0, 0, c)),
        out_shape=pltpu.HBM((OWNERS, 16, 1024), BF),
        compiler_params=SMALL,
    )(plan, lead, rest)


def lay_kernel(in_ref, out_ref):
    for cb in range(4):
        out_ref[:, :, cb * 256 : (cb + 1) * 256] = in_ref[:, cb]


def lay(arrived):
    out = pl.pallas_call(
        lay_kernel,
        grid=(KEY_VALUE_HEADS,),
        in_specs=[pl.BlockSpec((16, 4, 16, 256), lambda c: (0, 0, 0, c))],
        out_specs=pl.BlockSpec((16, 16, 1024), lambda c: (0, 0, c)),
        out_shape=jax.ShapeDtypeStruct((16, 16, 4096), BF),
        compiler_params=SMALL,
    )(arrived.reshape(16, 4, 16, 1024))
    return out.reshape(ROWS, 4096)


def swap(x):
    return lax.all_to_all(x, "dp", split_axis=0, concat_axis=0, tiled=True)


def per_device(bq, bk, bv, aq, ak, av, labels, plan):
    size = lax.axis_size("sp")
    bq, bk, bv, aq, ak, av = (t[0] for t in (bq, bk, bv, aq, ak, av))
    tables = tuple(jnp.asarray(t) for t in angle_tables())

    head = pack_lead(ak, av, labels)
    head1, head2 = (from_previous(head, size, s) for s in (1, 2))
    lab = (head, head1, head2)
    lead = attend(True, aq, 0, LEAD, lab, lab, tables)
    lead = swap(lead.reshape(OWNERS, 16, LEAD * 256))

    rest = pack(ak, av, LEAD)
    rest, _, _ = lax.optimization_barrier((rest, head1, head2))
    rest1, rest2 = (from_previous(rest, size, s) for s in (1, 2))
    others = KEY_VALUE_HEADS - LEAD
    other = attend(True, aq, LEAD, others, (rest, rest1, rest2), lab, tables, 30)
    other = swap(other.reshape(OWNERS, 16, others * 256))

    base = pack(bk, bv, 0)
    base1, base2 = (from_previous(base, size, s) for s in (1, 2))
    base_output = attend(False, bq, 0, KEY_VALUE_HEADS, (base, base1, base2), lab, tables)

    arrived = swap(pick(plan, lead, other))
    return base_output[None], lay(arrived)[None]


def solution(mesh):
    rows = P("dp", "sp", None)
    return jax.shard_map(
        per_device,
        mesh=mesh,
        in_specs=(rows, rows, rows, rows, rows, rows, P("dp", "sp"), P()),
        out_specs=(rows, rows),
        check_vma=False,
    )
```

```python
import functools
import math

import jax
import jax.numpy as jnp
import numpy as np
from jax import lax
from jax.experimental import pallas as pl
from jax.experimental.pallas import tpu as pltpu
from jax.sharding import PartitionSpec as P

QUERY_HEADS = 32
KEY_VALUE_HEADS = 4
HEAD_SIZE = 128
GROUP = QUERY_HEADS // KEY_VALUE_HEADS
SEGS = 3
THETA = 1000000.0
ROWS = 256
OWNERS = 64
LEAD = 1
SCALE = math.log2(math.e) / math.sqrt(HEAD_SIZE)
MASKED = -1e30
BF = jnp.bfloat16
F32 = jnp.float32
SMALL = pltpu.CompilerParams(vmem_limit_bytes=16 << 20)


def in_hbm(x):
    return pltpu.with_memory_space_constraint(x, pltpu.HBM)


def angle_tables():
    half = HEAD_SIZE // 2
    rate = THETA ** (-2.0 * np.arange(half) / HEAD_SIZE)
    angle = np.arange(3 * ROWS)[:, None] * np.concatenate([rate, rate])[None, :]
    return np.cos(angle).astype(np.float32), np.sin(angle).astype(np.float32)


def pack_lead_kernel(k_ref, v_ref, lab_ref, out_ref):
    width = LEAD * 256
    for c in range(LEAD):
        out_ref[0:ROWS, c * 256 : c * 256 + 128] = k_ref[:, c * 128 : (c + 1) * 128]
        out_ref[0:ROWS, c * 256 + 128 : c * 256 + 256] = v_ref[:, c * 128 : (c + 1) * 128]
    along = (lab_ref[...] + 1).astype(F32)
    down = jnp.transpose(jnp.broadcast_to(along, (128, ROWS)))
    out_ref[0:ROWS, width : width + 128] = down.astype(BF)
    out_ref[ROWS : ROWS + 16, ROWS:] = jnp.zeros((16, width + 128 - ROWS), BF)
    out_ref[ROWS : ROWS + 16, 0:ROWS] = jnp.broadcast_to(along, (16, ROWS)).astype(BF)


def pack_lead(k, v, labels):
    half = pl.BlockSpec((ROWS, LEAD * 128), lambda i: (0, 0))
    return pl.pallas_call(
        pack_lead_kernel,
        grid=(1,),
        in_specs=[half, half, pl.BlockSpec((1, ROWS), lambda i: (0, 0))],
        out_specs=pl.BlockSpec((ROWS + 16, LEAD * 256 + 128), lambda i: (0, 0)),
        out_shape=jax.ShapeDtypeStruct((ROWS + 16, LEAD * 256 + 128), BF),
        compiler_params=SMALL,
    )(in_hbm(k), in_hbm(v), in_hbm(labels))


def pack_kernel(first, k_ref, v_ref, out_ref):
    for i, c in enumerate(range(first, KEY_VALUE_HEADS)):
        out_ref[:, i * 256 : i * 256 + 128] = k_ref[:, c * 128 : (c + 1) * 128]
        out_ref[:, i * 256 + 128 : i * 256 + 256] = v_ref[:, c * 128 : (c + 1) * 128]


def pack(k, v, first):
    return pl.pallas_call(
        functools.partial(pack_kernel, first),
        out_shape=jax.ShapeDtypeStruct((ROWS, (KEY_VALUE_HEADS - first) * 256), BF),
        compiler_params=SMALL,
    )(in_hbm(k), in_hbm(v))


def from_previous(x, size, step):
    return lax.ppermute(x, "sp", [(i, (i + step) % size) for i in range(size)])


def rotate(x, cosine, sine):
    x = x.astype(F32)
    return (x * cosine + pltpu.roll(x, HEAD_SIZE // 2, 1) * sine).astype(BF)


def attend_kernel(
    pieces,
    place_ref,
    q_ref,
    kv0_ref,
    kv1_ref,
    kv2_ref,
    down0_ref,
    down1_ref,
    down2_ref,
    along0_ref,
    along1_ref,
    along2_ref,
    cos_ref,
    sin_ref,
    out_ref,
    turn_cos,
    turn_sin,
    bias_near,
    bias_ends,
):
    within = lax.broadcasted_iota(jnp.int32, (ROWS, ROWS), 1) <= lax.broadcasted_iota(
        jnp.int32, (ROWS, ROWS), 0
    )

    @pl.when(pl.program_id(0) == 0)
    def _():
        along = [ref[0:1, :].astype(F32) for ref in (along2_ref, along1_ref, along0_ref)]
        down = [ref[...].astype(F32) for ref in (down2_ref, down1_ref, down0_ref)]
        back = [jnp.where(place_ref[0] >= n, 1.0, 0.0) for n in (2, 1)]
        along = [along[0] * back[0], along[1] * back[1], along[2]]
        down = [down[0] * back[0], down[1] * back[1], down[2]]
        place = lax.broadcasted_iota(jnp.int32, (1, ROWS), 1)
        starts = []
        for label in range(1, SEGS + 1):
            least = jnp.full((1, ROWS), 3 * ROWS - 1, jnp.int32)
            for b in range(3):
                least = jnp.minimum(
                    least, jnp.where(along[b] == label, place + b * ROWS, 3 * ROWS - 1)
                )
            starts.append(jnp.min(least))
        start_cos = [cos_ref[pl.ds(s, 1), :] for s in starts]
        start_sin = [sin_ref[pl.ds(s, 1), :] for s in starts]
        sign = jnp.where(
            lax.broadcasted_iota(jnp.int32, (1, HEAD_SIZE), 1) < HEAD_SIZE // 2, -1.0, 1.0
        )
        for b in range(3):
            rows = pl.ds(b * ROWS, ROWS)
            first, second = down[b] == 1, down[b] == 2
            sc = jnp.where(first, start_cos[0], jnp.where(second, start_cos[1], start_cos[2]))
            ss = jnp.where(first, start_sin[0], jnp.where(second, start_sin[1], start_sin[2]))
            ic, isn = cos_ref[rows, :], sin_ref[rows, :]
            turn_cos[rows, :] = ic * sc + isn * ss
            turn_sin[rows, :] = (isn * sc - ic * ss) * sign
        own = jnp.concatenate([down[2], down[2]], axis=1)
        bias_near[...] = jnp.where(along[1] == own, 0.0, MASKED)
        bias_ends[...] = jnp.where(jnp.where(within, along[2], along[0]) == own, 0.0, MASKED)

    keys, values = [], []
    ones = jnp.ones((ROWS, HEAD_SIZE), BF)
    for b, ref in enumerate((kv2_ref, kv1_ref, kv0_ref)):
        rows = pl.ds(b * ROWS, ROWS)
        keys.append(rotate(ref[0:ROWS, 0:128], turn_cos[rows, :], turn_sin[rows, :]))
        values.append(jnp.concatenate([ref[0:ROWS, 128:256], ones], axis=1))
    keys = jnp.concatenate(keys, axis=0)
    values = jnp.concatenate(values, axis=0)
    own_cos = turn_cos[pl.ds(2 * ROWS, ROWS), :]
    own_sin = turn_sin[pl.ds(2 * ROWS, ROWS), :]
    for h in range(GROUP):
        q = rotate(q_ref[:, h * 128 : (h + 1) * 128], own_cos, own_sin)
        s = lax.dot_general(q, keys, (((1,), (1,)), ((), ())), preferred_element_type=F32)
        ends = jnp.where(within, s[:, 2 * ROWS :], s[:, :ROWS]) * SCALE + bias_ends[...]
        near = s[:, ROWS : 2 * ROWS] * SCALE + bias_near[...]
        peak = jnp.max(jnp.maximum(ends, near), axis=1, keepdims=True)
        ends = jnp.exp2(ends - peak)
        near = jnp.exp2(near - peak).astype(BF)
        inner = jnp.where(within, ends, 0.0).astype(BF)
        outer = jnp.where(within, 0.0, ends).astype(BF)
        weights = jnp.concatenate([outer, near, inner], axis=1)
        o = jnp.dot(weights, values, preferred_element_type=F32)
        o = (o[:, :128] / o[:, 128:]).astype(BF)
        if pieces:
            lanes = slice((h % 2) * 128, (h % 2) * 128 + 128)
            out_ref[:, h // 2, :, lanes] = o.reshape(16, 16, 128)
        else:
            out_ref[:, h * 128 : (h + 1) * 128] = o


def attend(pieces, q, first, count, kvs, lab, tables, weight=1):
    width = LEAD * 256
    specs = [pl.BlockSpec(memory_space=pltpu.SMEM)]
    specs += [pl.BlockSpec((ROWS, GROUP * 128), lambda c: (0, c + first))]
    specs += [pl.BlockSpec((ROWS, 256), lambda c: (0, c))] * 3
    specs += [pl.BlockSpec((ROWS, 128), lambda c: (0, width // 128))] * 3
    specs += [pl.BlockSpec((16, ROWS), lambda c: (ROWS // 16, 0))] * 3
    specs += [pl.BlockSpec((3 * ROWS, HEAD_SIZE), lambda c: (0, 0))] * 2
    if pieces:
        out_shape = pltpu.HBM((16, 4, 16, count * 256), BF)
        out_spec = pl.BlockSpec((16, 4, 16, 256), lambda c: (0, 0, 0, c))
    else:
        out_shape = jax.ShapeDtypeStruct((ROWS, QUERY_HEADS * HEAD_SIZE), BF)
        out_spec = pl.BlockSpec((ROWS, GROUP * 128), lambda c: (0, c + first))
    return pl.pallas_call(
        functools.partial(attend_kernel, pieces),
        grid=(count,),
        in_specs=specs,
        out_specs=out_spec,
        out_shape=out_shape,
        scratch_shapes=[
            pltpu.VMEM((3 * ROWS, HEAD_SIZE), F32),
            pltpu.VMEM((3 * ROWS, HEAD_SIZE), F32),
            pltpu.VMEM((ROWS, ROWS), F32),
            pltpu.VMEM((ROWS, ROWS), F32),
        ],
        compiler_params=pltpu.CompilerParams(vmem_limit_bytes=32 << 20),
        cost_estimate=pl.CostEstimate(
            flops=weight * count * GROUP * 4 * ROWS * 3 * ROWS * HEAD_SIZE,
            bytes_accessed=count * ROWS * (GROUP * 256 * 2 + 3 * 512),
            transcendentals=count * GROUP * ROWS * 2 * ROWS,
        ),
    )(lax.axis_index("sp").astype(jnp.int32)[None], in_hbm(q), *kvs, *lab, *lab, *(in_hbm(t) for t in tables))


def pick_kernel(plan_ref, lead_ref, rest_ref, out_ref, source, stage, sems):
    width = LEAD * 256
    part = OWNERS // 4

    def note(u, carry):
        source[plan_ref[u]] = u
        return carry

    lax.fori_loop(0, OWNERS, note, 0, unroll=8)
    copies = []
    for p in range(4):
        def one(i, carry, p=p):
            u = source[p * part + i]
            stage[p, i, :, 0:width] = lead_ref[u]
            stage[p, i, :, width:] = rest_ref[u]
            return carry

        lax.fori_loop(0, part, one, 0, unroll=4)
        copies.append(
            pltpu.make_async_copy(stage.at[p], out_ref.at[pl.ds(p * part, part)], sems.at[p])
        )
        copies[-1].start()
    for copy in copies:
        copy.wait()


def pick(plan, lead, rest):
    whole = pl.BlockSpec(memory_space=pltpu.VMEM)
    return pl.pallas_call(
        pick_kernel,
        in_specs=[pl.BlockSpec(memory_space=pltpu.SMEM), whole, whole],
        out_specs=pl.BlockSpec(memory_space=pl.ANY),
        out_shape=pltpu.HBM((OWNERS, 16, 1024), BF),
        scratch_shapes=[
            pltpu.SMEM((OWNERS,), jnp.int32),
            pltpu.VMEM((4, OWNERS // 4, 16, 1024), BF),
            pltpu.SemaphoreType.DMA((4,)),
        ],
        compiler_params=SMALL,
    )(plan, lead, rest)


def lay_kernel(in_ref, out_ref, sems):
    copies = []
    for c in range(KEY_VALUE_HEADS):
        for cb in range(4):
            copies.append(
                pltpu.make_async_copy(
                    in_ref.at[:, cb, :, pl.ds(c * 256, 256)],
                    out_ref.at[:, :, pl.ds(c * 1024 + cb * 256, 256)],
                    sems.at[c * 4 + cb],
                )
            )
    for copy in copies:
        copy.start()
    for copy in copies:
        copy.wait()


def lay(arrived):
    out = pl.pallas_call(
        lay_kernel,
        in_specs=[pl.BlockSpec(memory_space=pltpu.VMEM)],
        out_specs=pl.BlockSpec(memory_space=pl.ANY),
        out_shape=pltpu.HBM((16, 16, 4096), BF),
        scratch_shapes=[pltpu.SemaphoreType.DMA((16,))],
        compiler_params=SMALL,
    )(arrived.reshape(16, 4, 16, 1024))
    return out.reshape(ROWS, 4096)


def swap(x):
    return lax.all_to_all(x, "dp", split_axis=0, concat_axis=0, tiled=True)


def per_device(bq, bk, bv, aq, ak, av, labels, plan):
    size = lax.axis_size("sp")
    bq, bk, bv, aq, ak, av = (t[0] for t in (bq, bk, bv, aq, ak, av))
    tables = tuple(jnp.asarray(t) for t in angle_tables())

    head = pack_lead(ak, av, labels)
    head1, head2 = (from_previous(head, size, s) for s in (1, 2))
    lab = (head, head1, head2)
    lead = attend(True, aq, 0, LEAD, lab, lab, tables)
    lead = swap(lead.reshape(OWNERS, 16, LEAD * 256))

    rest = pack(ak, av, LEAD)
    rest, _, _ = lax.optimization_barrier((rest, head1, head2))
    rest1, rest2 = (from_previous(rest, size, s) for s in (1, 2))
    others = KEY_VALUE_HEADS - LEAD
    other = attend(True, aq, LEAD, others, (rest, rest1, rest2), lab, tables, 30)
    other = swap(other.reshape(OWNERS, 16, others * 256))

    base = pack(bk, bv, 0)
    base1, base2 = (from_previous(base, size, s) for s in (1, 2))
    base_output = attend(False, bq, 0, KEY_VALUE_HEADS, (base, base1, base2), lab, tables)

    arrived = swap(pick(plan, lead, other))
    return base_output[None], lay(arrived)[None]


def solution(mesh):
    rows = P("dp", "sp", None)
    return jax.shard_map(
        per_device,
        mesh=mesh,
        in_specs=(rows, rows, rows, rows, rows, rows, P("dp", "sp"), P()),
        out_specs=(rows, rows),
        check_vma=False,
    )
```

```python
import functools
import math

import jax
import jax.numpy as jnp
import numpy as np
from jax import lax
from jax.experimental import pallas as pl
from jax.experimental.pallas import tpu as pltpu
from jax.sharding import PartitionSpec as P

QUERY_HEADS = 32
KEY_VALUE_HEADS = 4
HEAD_SIZE = 128
GROUP = QUERY_HEADS // KEY_VALUE_HEADS
SEGS = 3
THETA = 1000000.0
ROWS = 256
OWNERS = 64
LEAD = 1
SCALE = math.log2(math.e) / math.sqrt(HEAD_SIZE)
MASKED = -1e30
BF = jnp.bfloat16
F32 = jnp.float32
SMALL = pltpu.CompilerParams(vmem_limit_bytes=16 << 20)


def in_hbm(x):
    return pltpu.with_memory_space_constraint(x, pltpu.HBM)


def angle_tables():
    half = HEAD_SIZE // 2
    rate = THETA ** (-2.0 * np.arange(half) / HEAD_SIZE)
    angle = np.arange(3 * ROWS)[:, None] * np.concatenate([rate, rate])[None, :]
    return np.cos(angle).astype(np.float32), np.sin(angle).astype(np.float32)


def pack_lead_kernel(k_ref, v_ref, lab_ref, out_ref):
    width = LEAD * 256
    for c in range(LEAD):
        out_ref[0:ROWS, c * 256 : c * 256 + 128] = k_ref[:, c * 128 : (c + 1) * 128]
        out_ref[0:ROWS, c * 256 + 128 : c * 256 + 256] = v_ref[:, c * 128 : (c + 1) * 128]
    along = (lab_ref[...] + 1).astype(F32)
    down = jnp.transpose(jnp.broadcast_to(along, (128, ROWS)))
    out_ref[0:ROWS, width : width + 128] = down.astype(BF)
    out_ref[ROWS : ROWS + 16, ROWS:] = jnp.zeros((16, width + 128 - ROWS), BF)
    out_ref[ROWS : ROWS + 16, 0:ROWS] = jnp.broadcast_to(along, (16, ROWS)).astype(BF)


def pack_lead(k, v, labels):
    half = pl.BlockSpec((ROWS, LEAD * 128), lambda i: (0, 0))
    return pl.pallas_call(
        pack_lead_kernel,
        grid=(1,),
        in_specs=[half, half, pl.BlockSpec((1, ROWS), lambda i: (0, 0))],
        out_specs=pl.BlockSpec((ROWS + 16, LEAD * 256 + 128), lambda i: (0, 0)),
        out_shape=jax.ShapeDtypeStruct((ROWS + 16, LEAD * 256 + 128), BF),
        compiler_params=SMALL,
    )(in_hbm(k), in_hbm(v), in_hbm(labels))


def pack_kernel(first, k_ref, v_ref, out_ref):
    for i, c in enumerate(range(first, KEY_VALUE_HEADS)):
        out_ref[:, i * 256 : i * 256 + 128] = k_ref[:, c * 128 : (c + 1) * 128]
        out_ref[:, i * 256 + 128 : i * 256 + 256] = v_ref[:, c * 128 : (c + 1) * 128]


def pack(k, v, first):
    return pl.pallas_call(
        functools.partial(pack_kernel, first),
        out_shape=jax.ShapeDtypeStruct((ROWS, (KEY_VALUE_HEADS - first) * 256), BF),
        compiler_params=SMALL,
    )(in_hbm(k), in_hbm(v))


def from_previous(x, size, step):
    return lax.ppermute(x, "sp", [(i, (i + step) % size) for i in range(size)])


def rotate(x, cosine, sine):
    x = x.astype(F32)
    return (x * cosine + pltpu.roll(x, HEAD_SIZE // 2, 1) * sine).astype(BF)


def attend_kernel(
    pieces,
    place_ref,
    q_ref,
    kv0_ref,
    kv1_ref,
    kv2_ref,
    down0_ref,
    down1_ref,
    down2_ref,
    along0_ref,
    along1_ref,
    along2_ref,
    cos_ref,
    sin_ref,
    out_ref,
    turn_cos,
    turn_sin,
    bias_near,
    bias_ends,
):
    within = lax.broadcasted_iota(jnp.int32, (ROWS, ROWS), 1) <= lax.broadcasted_iota(
        jnp.int32, (ROWS, ROWS), 0
    )

    @pl.when(pl.program_id(0) == 0)
    def _():
        along = [ref[0:1, :].astype(F32) for ref in (along2_ref, along1_ref, along0_ref)]
        down = [ref[...].astype(F32) for ref in (down2_ref, down1_ref, down0_ref)]
        back = [jnp.where(place_ref[0] >= n, 1.0, 0.0) for n in (2, 1)]
        along = [along[0] * back[0], along[1] * back[1], along[2]]
        down = [down[0] * back[0], down[1] * back[1], down[2]]
        place = lax.broadcasted_iota(jnp.int32, (1, ROWS), 1)
        starts = []
        for label in range(1, SEGS + 1):
            least = jnp.full((1, ROWS), 3 * ROWS - 1, jnp.int32)
            for b in range(3):
                least = jnp.minimum(
                    least, jnp.where(along[b] == label, place + b * ROWS, 3 * ROWS - 1)
                )
            starts.append(jnp.min(least))
        start_cos = [cos_ref[pl.ds(s, 1), :] for s in starts]
        start_sin = [sin_ref[pl.ds(s, 1), :] for s in starts]
        sign = jnp.where(
            lax.broadcasted_iota(jnp.int32, (1, HEAD_SIZE), 1) < HEAD_SIZE // 2, -1.0, 1.0
        )
        for b in range(3):
            rows = pl.ds(b * ROWS, ROWS)
            first, second = down[b] == 1, down[b] == 2
            sc = jnp.where(first, start_cos[0], jnp.where(second, start_cos[1], start_cos[2]))
            ss = jnp.where(first, start_sin[0], jnp.where(second, start_sin[1], start_sin[2]))
            ic, isn = cos_ref[rows, :], sin_ref[rows, :]
            turn_cos[rows, :] = ic * sc + isn * ss
            turn_sin[rows, :] = (isn * sc - ic * ss) * sign
        own = jnp.concatenate([down[2], down[2]], axis=1)
        bias_near[...] = jnp.where(along[1] == own, 0.0, MASKED)
        bias_ends[...] = jnp.where(jnp.where(within, along[2], along[0]) == own, 0.0, MASKED)

    keys, values = [], []
    ones = jnp.ones((ROWS, HEAD_SIZE), BF)
    for b, ref in enumerate((kv2_ref, kv1_ref, kv0_ref)):
        rows = pl.ds(b * ROWS, ROWS)
        keys.append(rotate(ref[0:ROWS, 0:128], turn_cos[rows, :], turn_sin[rows, :]))
        values.append(jnp.concatenate([ref[0:ROWS, 128:256], ones], axis=1))
    keys = jnp.concatenate(keys, axis=0)
    values = jnp.concatenate(values, axis=0)
    own_cos = turn_cos[pl.ds(2 * ROWS, ROWS), :]
    own_sin = turn_sin[pl.ds(2 * ROWS, ROWS), :]
    for h in range(GROUP):
        q = rotate(q_ref[:, h * 128 : (h + 1) * 128], own_cos, own_sin)
        s = lax.dot_general(q, keys, (((1,), (1,)), ((), ())), preferred_element_type=F32)
        ends = jnp.where(within, s[:, 2 * ROWS :], s[:, :ROWS]) * SCALE + bias_ends[...]
        near = s[:, ROWS : 2 * ROWS] * SCALE + bias_near[...]
        peak = jnp.max(jnp.maximum(ends, near), axis=1, keepdims=True)
        ends = jnp.exp2(ends - peak)
        near = jnp.exp2(near - peak).astype(BF)
        inner = jnp.where(within, ends, 0.0).astype(BF)
        outer = jnp.where(within, 0.0, ends).astype(BF)
        weights = jnp.concatenate([outer, near, inner], axis=1)
        o = jnp.dot(weights, values, preferred_element_type=F32)
        o = (o[:, :128] / o[:, 128:]).astype(BF)
        if pieces:
            lanes = slice((h % 2) * 128, (h % 2) * 128 + 128)
            out_ref[:, h // 2, :, lanes] = o.reshape(16, 16, 128)
        else:
            out_ref[:, h * 128 : (h + 1) * 128] = o


def attend(pieces, q, first, count, kvs, lab, tables, weight=1):
    width = LEAD * 256
    specs = [pl.BlockSpec(memory_space=pltpu.SMEM)]
    specs += [pl.BlockSpec((ROWS, GROUP * 128), lambda c: (0, c + first))]
    specs += [pl.BlockSpec((ROWS, 256), lambda c: (0, c))] * 3
    specs += [pl.BlockSpec((ROWS, 128), lambda c: (0, width // 128))] * 3
    specs += [pl.BlockSpec((16, ROWS), lambda c: (ROWS // 16, 0))] * 3
    specs += [pl.BlockSpec((3 * ROWS, HEAD_SIZE), lambda c: (0, 0))] * 2
    if pieces:
        out_shape = pltpu.HBM((16, 4, 16, count * 256), BF)
        out_spec = pl.BlockSpec((16, 4, 16, 256), lambda c: (0, 0, 0, c))
    else:
        out_shape = jax.ShapeDtypeStruct((ROWS, QUERY_HEADS * HEAD_SIZE), BF)
        out_spec = pl.BlockSpec((ROWS, GROUP * 128), lambda c: (0, c + first))
    return pl.pallas_call(
        functools.partial(attend_kernel, pieces),
        grid=(count,),
        in_specs=specs,
        out_specs=out_spec,
        out_shape=out_shape,
        scratch_shapes=[
            pltpu.VMEM((3 * ROWS, HEAD_SIZE), F32),
            pltpu.VMEM((3 * ROWS, HEAD_SIZE), F32),
            pltpu.VMEM((ROWS, ROWS), F32),
            pltpu.VMEM((ROWS, ROWS), F32),
        ],
        compiler_params=pltpu.CompilerParams(vmem_limit_bytes=32 << 20),
        cost_estimate=pl.CostEstimate(
            flops=weight * count * GROUP * 4 * ROWS * 3 * ROWS * HEAD_SIZE,
            bytes_accessed=count * ROWS * (GROUP * 256 * 2 + 3 * 512),
            transcendentals=count * GROUP * ROWS * 2 * ROWS,
        ),
    )(lax.axis_index("sp").astype(jnp.int32)[None], in_hbm(q), *kvs, *lab, *lab, *(in_hbm(t) for t in tables))


def pick_kernel(plan_ref, lead_ref, rest_ref, out_ref, source, stage, sems):
    width = LEAD * 256
    part = OWNERS // 4

    def note(u, carry):
        source[plan_ref[u]] = u
        return carry

    lax.fori_loop(0, OWNERS, note, 0, unroll=8)
    copies = []
    for p in range(4):
        def one(i, carry, p=p):
            u = source[p * part + i]
            stage[p, i, :, 0:width] = lead_ref[u]
            stage[p, i, :, width:] = rest_ref[u]
            return carry

        lax.fori_loop(0, part, one, 0, unroll=4)
        copies.append(
            pltpu.make_async_copy(stage.at[p], out_ref.at[pl.ds(p * part, part)], sems.at[p])
        )
        copies[-1].start()
    for copy in copies:
        copy.wait()


def pick(plan, lead, rest):
    whole = pl.BlockSpec(memory_space=pltpu.VMEM)
    return pl.pallas_call(
        pick_kernel,
        in_specs=[pl.BlockSpec(memory_space=pltpu.SMEM), whole, whole],
        out_specs=pl.BlockSpec(memory_space=pl.ANY),
        out_shape=pltpu.HBM((OWNERS, 16, 1024), BF),
        scratch_shapes=[
            pltpu.SMEM((OWNERS,), jnp.int32),
            pltpu.VMEM((4, OWNERS // 4, 16, 1024), BF),
            pltpu.SemaphoreType.DMA((4,)),
        ],
        compiler_params=SMALL,
    )(plan, lead, rest)


def lay_kernel(in_ref, out_ref, sems):
    copies = []
    for c in range(KEY_VALUE_HEADS):
        for cb in range(4):
            copies.append(
                pltpu.make_async_copy(
                    in_ref.at[:, cb, :, pl.ds(c * 256, 256)],
                    out_ref.at[:, :, pl.ds(c * 1024 + cb * 256, 256)],
                    sems.at[c * 4 + cb],
                )
            )
    for copy in copies:
        copy.start()
    for copy in copies:
        copy.wait()


def lay(arrived):
    out = pl.pallas_call(
        lay_kernel,
        in_specs=[pl.BlockSpec(memory_space=pltpu.VMEM)],
        out_specs=pl.BlockSpec(memory_space=pl.ANY),
        out_shape=pltpu.HBM((16, 16, 4096), BF),
        scratch_shapes=[pltpu.SemaphoreType.DMA((16,))],
        compiler_params=SMALL,
    )(arrived.reshape(16, 4, 16, 1024))
    return out.reshape(ROWS, 4096)


def swap(x):
    return lax.all_to_all(x, "dp", split_axis=0, concat_axis=0, tiled=True)


def per_device(bq, bk, bv, aq, ak, av, labels, plan):
    size = lax.axis_size("sp")
    bq, bk, bv, aq, ak, av = (t[0] for t in (bq, bk, bv, aq, ak, av))
    tables = tuple(jnp.asarray(t) for t in angle_tables())

    head = pack_lead(ak, av, labels)
    head1, head2 = (from_previous(head, size, s) for s in (1, 2))
    lab = (head, head1, head2)
    lead = attend(True, aq, 0, LEAD, lab, lab, tables)
    lead = swap(lead.reshape(OWNERS, 16, LEAD * 256))

    rest = pack(ak, av, LEAD)
    rest, _ = lax.optimization_barrier((rest, head))
    rest1, rest2 = (from_previous(rest, size, s) for s in (1, 2))
    others = KEY_VALUE_HEADS - LEAD
    other = attend(True, aq, LEAD, others, (rest, rest1, rest2), lab, tables, 4)
    other = swap(other.reshape(OWNERS, 16, others * 256))

    base = pack(bk, bv, 0)
    base1, base2 = (from_previous(base, size, s) for s in (1, 2))
    base_output = attend(False, bq, 0, KEY_VALUE_HEADS, (base, base1, base2), lab, tables)

    arrived = swap(pick(plan, lead, other))
    return base_output[None], lay(arrived)[None]


def solution(mesh):
    rows = P("dp", "sp", None)
    return jax.shard_map(
        per_device,
        mesh=mesh,
        in_specs=(rows, rows, rows, rows, rows, rows, P("dp", "sp"), P()),
        out_specs=(rows, rows),
        check_vma=False,
    )
```
